32 devices in a mesh: slab: 8 (over z, x), mode: 4 (over y, core).
Axes of the slice: x: 2, y: 2, z: 4, core: 2. Of those that a mesh axis runs over, the one named last changes fastest.
Arguments:
- design: float32 [16, 128, 128], P('slab', 'mode'), may hold values from 0.03 to 1
- mode_shapes: float32 [4, 3, 16, 128, 128], P('mode', None, 'slab'), may hold values from -2.4 to 2.4
- eigenvalues: float32 [4], P('mode'), may hold values from 0.5 to 2
Outputs:
- sensitivity: float32 [16, 128, 128], P('slab', 'mode')
- new_design: float32 [16, 128, 128], P('slab', 'mode')
The draws below stay inside these ranges and needn't reach their ends.
All inputs are finite; a program needn't handle non-finite values.
Results may differ from the reference program's by a relative error of at most 0.0003.
Values sent between devices are 32-bit elements; how exact they have to be, the bound alone decides.
A program may use at most 64 MiB of HBM per device.

```python
import math
import jax
import jax.numpy as jnp
import numpy as np
from jax import lax

NY = 128
NZ = 128
FR = 3
BISECT = 12
MODES = 4
NX = 16


def draw_design(key, part):
    across = jnp.arange(NX, dtype=jnp.float32) / NX
    along_rows = jnp.arange(NY, dtype=jnp.float32) / NY
    trend = 0.33 + 0.335 * (across[:, None, None] + along_rows[None, :, None])
    rough = jax.random.uniform(key, (NX, NY, NZ), jnp.float32, 0.1, 1.0)
    return trend * rough


def shard_levels(own_key, dims, cuts, least, top_value):
    level, own = 1.0, jax.random.fold_in(own_key, 6)
    for axis_at, parts in cuts:
        heights = jnp.exp(jax.random.uniform(jax.random.fold_in(own, axis_at), (parts,), jnp.float32, least / len(cuts), top_value / len(cuts)))
        level = level * jnp.repeat(heights, dims[axis_at] // parts).reshape([-1 if axis == axis_at else 1 for axis in range(len(dims))])
    return level


def gaussian(rng, dims, scale, reach, shards=(), kind=jnp.bfloat16):
    level = shard_levels(rng, dims, shards, -0.22, 0.18) if shards else 1.0
    values = jax.random.normal(rng, dims, jnp.float32) * scale * level
    return jnp.minimum(jnp.maximum(values, -reach), reach).astype(kind)


def setup_inputs(seed: int = 0) -> dict:
    streams_of = jax.random.split(jax.random.key(seed), 4)
    return {
        "design": draw_design(jax.random.fold_in(streams_of[3], 71), 0),
        "mode_shapes": gaussian(streams_of[1], (MODES, 3, NX, NY, NZ), 0.3, 2.4, ((0, 4), (2, 8)), jnp.float32),
        "eigenvalues": jnp.clip(jnp.exp(math.log(2.0) - 1.3862944 * jax.random.uniform(streams_of[2], (MODES,), jnp.float32) ** shard_levels(streams_of[2], (MODES,), ((0, 4),), -0.2, 0.2)), 0.5, 2.0),
    }


KS_SHARP = 2.0
PENALTY = 3.0
FLOOR_MODULUS = 0.001
MOVE_LIMIT = 0.2
POISSON = 0.3
LEVEL_LOW = -14.0
LEVEL_HIGH = 14.0

def element_tables():
    lame_first = POISSON / ((1.0 + POISSON) * (1.0 - 2.0 * POISSON))
    shear_modulus = 0.5 / (1.0 + POISSON)
    elastic = np.zeros((6, 6))
    elastic[:3, :3] = lame_first
    for i in range(3):
        elastic[i, i] += 2.0 * shear_modulus
        elastic[i + 3, i + 3] = shear_modulus
    corner_signs = np.array([[a, b, c] for a in (0, 1) for b in (0, 1) for c in (0, 1)]) * 2.0 - 1.0
    gauss_points = [-1.0 / np.sqrt(3.0), 1.0 / np.sqrt(3.0)]
    stiffness = np.zeros((24, 24))
    mass_matrix = np.zeros((24, 24))
    for first in gauss_points:
        for second in gauss_points:
            for third in gauss_points:
                sample = np.array([first, second, third])
                factors = 1.0 + corner_signs * sample
                shape_values = np.prod(factors, axis=1) / 8.0
                gradients = np.zeros((8, 3))
                for d in range(3):
                    others = [e for e in range(3) if e != d]
                    gradients[:, d] = corner_signs[:, d] * factors[:, others[0]] * factors[:, others[1]] / 4.0
                strain = np.zeros((6, 24))
                shape_rows = np.zeros((3, 24))
                for n in range(8):
                    strain[0, 3 * n] = gradients[n, 0]
                    strain[1, 3 * n + 1] = gradients[n, 1]
                    strain[2, 3 * n + 2] = gradients[n, 2]
                    strain[3, 3 * n] = gradients[n, 1]
                    strain[3, 3 * n + 1] = gradients[n, 0]
                    strain[4, 3 * n + 1] = gradients[n, 2]
                    strain[4, 3 * n + 2] = gradients[n, 1]
                    strain[5, 3 * n] = gradients[n, 2]
                    strain[5, 3 * n + 2] = gradients[n, 0]
                    for i in range(3):
                        shape_rows[i, 3 * n + i] = shape_values[n]
                stiffness += strain.T @ elastic @ strain / 8.0
                mass_matrix += shape_rows.T @ shape_rows / 8.0
    return np.concatenate([stiffness, mass_matrix], 0)

def tent_valid(values, along):
    margin = FR - 1
    length = values.shape[along] - 2 * margin
    summed = None
    for offset in range(-margin, margin + 1):
        shifted = (FR - abs(offset)) * lax.slice_in_dim(values, margin + offset, margin + offset + length, axis=along)
        summed = shifted if summed is None else summed + shifted
    return summed

def tent_padded(values, along):
    margin = FR - 1
    widths = [(0, 0)] * values.ndim
    widths[along] = (margin, margin)
    return tent_valid(jnp.pad(values, widths), along)

def smooth(values):
    return tent_padded(tent_padded(tent_padded(values, 2), 0), 1)

def update(design, sensitivity, measure, level):
    factor = jnp.sqrt(jnp.maximum(sensitivity, 0.0) / (jnp.exp(level) * measure))
    return jnp.clip(design * factor, jnp.maximum(design - MOVE_LIMIT, 0.0), jnp.minimum(design + MOVE_LIMIT, 1.0))

def element_forms(node_values, tables):
    padded = jnp.pad(node_values, ((0, 0), (0, 1), (0, 1), (0, 1)))

    def one_layer(position):
        planes = lax.dynamic_slice_in_dim(padded, position, 2, 1)
        corners = []
        for a in (0, 1):
            for b in (0, 1):
                for c in (0, 1):
                    corners.append(planes[:, a, b:b + NY, c:c + NZ])
        stacked = jnp.stack(corners, 0).reshape(24, NY * NZ)
        product = jnp.dot(tables, stacked, precision=lax.Precision.HIGHEST)
        stiff_form = lax.optimization_barrier(jnp.sum(product[:24] * stacked, 0)).reshape(NY, NZ)
        mass_form = lax.optimization_barrier(jnp.sum(product[24:] * stacked, 0)).reshape(NY, NZ)
        return (stiff_form, mass_form)
    return lax.map(one_layer, jnp.arange(NX, dtype=jnp.int32))

def reference(design, mode_shapes, eigenvalues):
    tables = jnp.asarray(element_tables(), jnp.float32)
    span = smooth(jnp.ones_like(design))
    density = smooth(design) / span
    target = jnp.sum(density)
    weights = jnp.exp(-KS_SHARP * eigenvalues)
    summed_weight = jnp.sum(weights)
    slope = PENALTY * (1.0 - FLOOR_MODULUS) * density * density

    def add_mode(number, partial_value):
        stiff_form, mass_form = element_forms(mode_shapes[number], tables)
        return partial_value + weights[number] * (slope * stiff_form - eigenvalues[number] * mass_form)
    partial_value = lax.fori_loop(0, MODES, add_mode, jnp.zeros_like(design))
    gradient = partial_value / summed_weight
    sensitivity = smooth(gradient / span)
    measure = smooth(1.0 / span)

    def halve(count, bounds):
        lower, upper = bounds
        middle = (lower + upper) * 0.5
        volume = jnp.sum(update(design, sensitivity, measure, middle) * measure)
        above = volume > target
        return (jnp.where(above, middle, lower), jnp.where(above, upper, middle))
    start = (jnp.asarray(LEVEL_LOW, jnp.float32), jnp.asarray(LEVEL_HIGH, jnp.float32))
    lower, upper = lax.fori_loop(0, BISECT, halve, start)
    new_design = update(design, sensitivity, measure, (lower + upper) * 0.5)
    return (sensitivity, new_design)
```

```python
import functools
import math

import jax
import jax.numpy as jnp
from jax import lax
from jax.experimental import pallas as pl
from jax.experimental.pallas import tpu as pltpu
from jax.sharding import PartitionSpec as P

FR = 3
BISECT = 12
KS_SHARP = 2.0
PENALTY = 3.0
FLOOR_MODULUS = 0.001
MOVE_LIMIT = 0.2
POISSON = 0.3
LEVEL_LOW = -14.0
LEVEL_HIGH = 14.0

MARGIN = FR - 1
PAD = 8
STEPS = BISECT // 2
TRIALS = 2**STEPS
LAME = POISSON / ((1.0 + POISSON) * (1.0 - 2.0 * POISSON))
SHEAR = 0.5 / (1.0 + POISSON)
MESH = pl.DeviceIdType.MESH
DIRECTIONS = [(dx, dy) for dx in (-1, 0, 1) for dy in (-1, 0, 1) if (dx, dy) != (0, 0)]


def edge_weight(position, count):
    total = jnp.zeros(position.shape, jnp.float32)
    for offset in range(-MARGIN, MARGIN + 1):
        inside = (position + offset >= 0) & (position + offset < count)
        total = total + jnp.where(inside, float(FR - abs(offset)), 0.0)
    return total


def axis_tables(position, count):
    measure = jnp.zeros(position.shape, jnp.float32)
    for offset in range(-MARGIN, MARGIN + 1):
        moved = position + offset
        inside = (moved >= 0) & (moved < count)
        weight = jnp.maximum(edge_weight(moved, count), 1.0)
        measure = measure + jnp.where(inside, float(FR - abs(offset)) / weight, 0.0)
    return edge_weight(position, count), measure


def filtered(ext, cells, rows, depth):
    lane = lax.broadcasted_iota(jnp.int32, (rows, depth), 1)
    results = []
    for cell in range(cells):
        along = None
        for offset in range(2 * MARGIN + 1):
            term = float(FR - abs(offset - MARGIN)) * ext[cell + offset]
            along = term if along is None else along + term
        total = None
        for offset in range(-MARGIN, MARGIN + 1):
            moved = pltpu.roll(along, (-offset) % (rows + 2 * PAD), 0) if offset else along
            term = float(FR - abs(offset)) * moved[PAD : PAD + rows]
            total = term if total is None else total + term
        value = float(FR) * total
        for offset in range(1, MARGIN + 1):
            after = jnp.where(lane < depth - offset, pltpu.roll(total, depth - offset, 1), 0.0)
            before = jnp.where(lane >= offset, pltpu.roll(total, offset, 1), 0.0)
            value = value + float(FR - offset) * (after + before)
        results.append(value)
    return results


def plane_parts(view, row, sub, node_rows, depth):
    after = row + sub
    following = view(pl.multiple_of(jnp.minimum(after, node_rows - 8), 8), 8)
    following = jnp.where(after < node_rows, following, jnp.zeros_like(following))
    value = jnp.concatenate([view(row, sub), following], 0)
    lane = lax.broadcasted_iota(jnp.int32, value.shape, 1)
    lifted = jnp.where(lane < depth - 1, pltpu.roll(value, depth - 1, 1), 0.0)
    parts = {}
    for z, base in ((0, value + lifted), (1, lifted - value)):
        above = pltpu.roll(base, sub + 7, 0)[:sub]
        parts[0, z] = base[:sub] + above
        parts[1, z] = above - base[:sub]
    return parts


def total_of(terms):
    result = terms[0]
    for term in terms[1:]:
        result = result + term
    return result


def energies(first, second):
    h = []
    for a, b in zip(first, second):
        h.append({(p, *key): (b[key] - a[key] if p else a[key] + b[key]) for p in (0, 1) for key in a})
    u, v, w = h
    sq = lambda value: value * value
    squares = [{key: sq(value) for key, value in comp.items()} for comp in h]
    su, sv, sw = squares
    q1 = su[1, 0, 0] + sv[0, 1, 0] + sw[0, 0, 1]
    q2 = total_of([su[1, 1, 0], su[1, 0, 1], sv[1, 1, 0], sv[0, 1, 1], sw[1, 0, 1], sw[0, 1, 1]])
    q3 = su[1, 1, 1] + sv[1, 1, 1] + sw[1, 1, 1]
    m0 = su[0, 0, 0] + sv[0, 0, 0] + sw[0, 0, 0]
    m1 = q1 + total_of([su[0, 1, 0], su[0, 0, 1], sv[1, 0, 0], sv[0, 0, 1], sw[1, 0, 0], sw[0, 1, 0]])
    m2 = q2 + total_of([su[0, 1, 1], sv[1, 0, 1], sw[1, 1, 0]])
    div0 = sq(u[1, 0, 0] + v[0, 1, 0] + w[0, 0, 1])
    div1 = sq(v[1, 1, 0] + w[1, 0, 1]) + sq(u[1, 1, 0] + w[0, 1, 1]) + sq(u[1, 0, 1] + v[0, 1, 1])
    cut0 = sq(u[0, 1, 0] + v[1, 0, 0]) + sq(u[0, 0, 1] + w[1, 0, 0]) + sq(v[0, 0, 1] + w[0, 1, 0])
    cut1 = sq(u[0, 1, 1] + v[1, 0, 1]) + sq(u[0, 1, 1] + w[1, 1, 0]) + sq(v[1, 0, 1] + w[1, 1, 0])
    stiff = (
        (LAME / 16.0) * div0
        + (SHEAR / 16.0) * (2.0 * q1 + cut0)
        + (LAME / 48.0) * div1
        + (SHEAR / 48.0) * (3.0 * q2 + cut1)
        + ((LAME + 4.0 * SHEAR) / 144.0) * q3
    )
    mass = (1.0 / 64.0) * m0 + (1.0 / 192.0) * m1 + (1.0 / 576.0) * m2 + (1.0 / 1728.0) * q3
    return stiff, mass


def kernel(
    slabs, groups,
    design_ref, shapes_ref, eig_ref, sens_ref, new_ref,
    design_ext, grad_ext, plane, outgoing, incoming, weight_tiles, partial, row_tiles, column_tiles, trial_rows,
    design_sems, grad_sems, plane_sems, form_sems, weight_sems, row_sems, column_sems,
):
    cells, rows, depth = design_ref.shape
    modes, node_rows = shapes_ref.shape[0], shapes_ref.shape[3]
    total_x, total_rows = cells * slabs, rows * groups
    s, m = lax.axis_index("slab"), lax.axis_index("mode")
    sub = 16 if rows % 16 == 0 else 8

    design_ext[...] = jnp.zeros_like(design_ext)
    grad_ext[...] = jnp.zeros_like(grad_ext)

    @pl.when(s == slabs - 1)
    def _():
        plane[...] = jnp.zeros_like(plane)

    barrier = pltpu.get_barrier_semaphore()
    expected = (groups - 1) + (slabs - 1)
    for d in range(1, groups):
        pl.semaphore_signal(barrier, inc=1, device_id=(s, lax.rem(m + d, groups)), device_id_type=MESH)
    for d in range(1, slabs):
        pl.semaphore_signal(barrier, inc=1, device_id=(lax.rem(s + d, slabs), m), device_id_type=MESH)
    for dx, dy in DIRECTIONS:
        if dx and dy:
            fits = (s + dx >= 0) & (s + dx < slabs) & (m + dy >= 0) & (m + dy < groups)
            expected = expected + fits.astype(jnp.int32)

            @pl.when(fits)
            def _():
                pl.semaphore_signal(barrier, inc=1, device_id=(s + dx, m + dy), device_id_type=MESH)

    pl.semaphore_wait(barrier, expected)

    def plane_copy():
        return pltpu.make_async_remote_copy(
            src_ref=shapes_ref.at[:, :, 0], dst_ref=plane,
            send_sem=plane_sems.at[0], recv_sem=plane_sems.at[1],
            device_id=(s - 1, m), device_id_type=MESH,
        )

    @pl.when(s > 0)
    def _():
        plane_copy().start()

    def halo(source, x_off, y_off, target, sems, number):
        dx, dy = DIRECTIONS[number]
        x_from, x_count, x_to = {
            1: (cells - MARGIN, MARGIN, 0), -1: (0, MARGIN, MARGIN + cells), 0: (0, cells, MARGIN)}[dx]
        y_from, y_count, y_to = {
            1: (rows - PAD, PAD, 0), -1: (0, PAD, PAD + rows), 0: (0, rows, PAD)}[dy]
        return pltpu.make_async_remote_copy(
            src_ref=source.at[pl.ds(x_off + x_from, x_count), pl.ds(y_off + y_from, y_count)],
            dst_ref=target.at[pl.ds(x_to, x_count), pl.ds(y_to, y_count)],
            send_sem=sems.at[0, number], recv_sem=sems.at[1, number],
            device_id=(s + dx, m + dy), device_id_type=MESH,
        )

    def each_halo(source, x_off, y_off, target, sems, action, sign):
        for number, (dx, dy) in enumerate(DIRECTIONS):
            x, y = s + sign * dx, m + sign * dy

            @pl.when((x >= 0) & (x < slabs) & (y >= 0) & (y < groups))
            def _():
                getattr(halo(source, x_off, y_off, target, sems, number), action)()

    design_halo = functools.partial(each_halo, design_ref, 0, 0, design_ext, design_sems)
    grad_halo = functools.partial(each_halo, grad_ext, MARGIN, PAD, grad_ext, grad_sems)

    weights = [jnp.exp(-KS_SHARP * jnp.full((8, depth), eig_ref[k])) for k in range(modes)]
    weight_tiles[m] = total_of(weights)

    def mode_exchange(buffer, sems):
        return [
            pltpu.make_async_remote_copy(
                src_ref=buffer.at[m], dst_ref=buffer.at[m],
                send_sem=sems.at[0, d], recv_sem=sems.at[1, d],
                device_id=(s, lax.rem(m + d, groups)), device_id_type=MESH,
            )
            for d in range(1, groups)
        ]

    def slab_exchange(buffer, sems):
        return [
            pltpu.make_async_remote_copy(
                src_ref=buffer.at[s], dst_ref=buffer.at[s],
                send_sem=sems.at[0, d], recv_sem=sems.at[1, d],
                device_id=(lax.rem(s + d, slabs), m), device_id_type=MESH,
            )
            for d in range(1, slabs)
        ]

    weight_copies = mode_exchange(weight_tiles, weight_sems)
    for copy in weight_copies:
        copy.start()
    design_halo("start", 1)

    def node_view(mode, comp, layer):
        if layer == cells:
            return lambda row, count: plane[mode, comp, pl.ds(row, count), :]
        return lambda row, count: shapes_ref[mode, comp, layer, pl.ds(row, count), :]

    def layer_forms(layer, group):
        def step(number, carry):
            row = pl.multiple_of(group * rows + number * sub, 8)
            stiff_sum = mass_sum = None
            for mode in range(modes):
                first, second = [
                    [plane_parts(node_view(mode, comp, at), row, sub, node_rows, depth) for comp in range(3)]
                    for at in (layer, layer + 1)
                ]
                stiff, mass = energies(first, second)
                weight = weights[mode][0:1]
                stiff = weight * stiff
                mass = (weight * eig_ref[mode]) * mass
                stiff_sum = stiff if mode == 0 else stiff_sum + stiff
                mass_sum = mass if mode == 0 else mass_sum + mass
            at = pl.multiple_of(number * sub, 8)
            outgoing[group, layer, 0, pl.ds(at, sub), :] = stiff_sum
            outgoing[group, layer, 1, pl.ds(at, sub), :] = mass_sum
            return carry

        lax.fori_loop(0, rows // sub, step, 0)

    def form_copy(layer, d):
        group = lax.rem(m + d, groups)
        return pltpu.make_async_remote_copy(
            src_ref=outgoing.at[group, layer], dst_ref=incoming.at[d, layer],
            send_sem=form_sems.at[0, layer, d], recv_sem=form_sems.at[1, layer, d],
            device_id=(s, group), device_id_type=MESH,
        )

    order = list(range(1, groups)) + [0]
    for layer in range(cells):
        if layer == cells - 1:
            design_ext[MARGIN : MARGIN + cells, PAD : PAD + rows, :] = design_ref[...]
            x_tables = [axis_tables(jnp.full((1, depth), s * cells + i, jnp.int32), total_x) for i in range(cells)]
            y_tables = axis_tables(m * rows + lax.broadcasted_iota(jnp.int32, (rows, depth), 0), total_rows)
            z_tables = axis_tables(lax.broadcasted_iota(jnp.int32, (1, depth), 1), depth)
            spans = [x[0] * (y_tables[0] * z_tables[0]) for x in x_tables]
            measures = [x[1] * (y_tables[1] * z_tables[1]) for x in x_tables]
            design_halo("wait_recv", -1)
            densities = [f / span for f, span in zip(filtered(design_ext, cells, rows, depth), spans)]

            @pl.when(s < slabs - 1)
            def _():
                plane_copy().wait_recv()

        for d in order:
            layer_forms(layer, lax.rem(m + d, groups))
            if d:
                form_copy(layer, d).start()

    for copy in weight_copies:
        copy.wait_recv()
    weight_total = total_of([weight_tiles[i] for i in range(groups)])[0:1]
    for cell in range(cells):
        stiff, mass = outgoing[m, cell, 0], outgoing[m, cell, 1]
        for d in range(1, groups):
            form_copy(cell, d).wait_recv()
            stiff = stiff + incoming[d, cell, 0]
            mass = mass + incoming[d, cell, 1]
        slope = PENALTY * (1.0 - FLOOR_MODULUS) * densities[cell] * densities[cell]
        gradient = (slope * stiff - mass) / weight_total
        grad_ext[MARGIN + cell, PAD : PAD + rows, :] = gradient / spans[cell]
    grad_halo("start", 1)
    grad_halo("wait_recv", -1)
    sensitivities = filtered(grad_ext, cells, rows, depth)

    lowers, uppers, scales = [], [], []
    for cell in range(cells):
        sensitivity, measure = sensitivities[cell], measures[cell]
        sens_ref[cell] = sensitivity
        design = design_ref[cell]
        scales.append(design * jnp.sqrt(jnp.maximum(sensitivity, 0.0) / measure) * measure)
        lowers.append(jnp.maximum(design - MOVE_LIMIT, 0.0) * measure)
        uppers.append(jnp.minimum(design + MOVE_LIMIT, 1.0) * measure)
    lower, upper, scale = [jnp.concatenate(parts, 0) for parts in (lowers, uppers, scales)]
    trial_rows[1] = lower
    trial_rows[2] = upper

    def folded(value):
        return jnp.sum(value, axis=0, keepdims=True)

    lane = lax.broadcasted_iota(jnp.int32, (8, depth), 1)
    low = jnp.full((1, 1), LEVEL_LOW, jnp.float32)
    target = None
    width = LEVEL_HIGH - LEVEL_LOW
    copies = []
    for turn in range(2):
        width = width / TRIALS
        trial_rows[0] = scale * jnp.exp(-0.5 * low)
        for trial in range(0, TRIALS, 8):
            lines = []
            for number in range(trial, trial + 8):
                if number == 0:
                    lines.append(folded(total_of(densities)))
                    continue
                factor = math.exp(-0.5 * width * number)
                lines.append(folded(jnp.minimum(jnp.maximum(trial_rows[0] * factor, trial_rows[1]), trial_rows[2])))
            partial[trial : trial + 8, :] = jnp.concatenate(lines, 0)
        if turn == 0:
            partial[TRIALS:, :] = jnp.zeros((partial.shape[0] - TRIALS, depth), jnp.float32)
        row_tiles[turn, m] = lax.dot_general(
            jnp.ones((8, depth), jnp.float32), partial[...], (((1,), (1,)), ((), ())),
            precision=lax.Precision.HIGHEST, preferred_element_type=jnp.float32,
        )
        across = mode_exchange(row_tiles.at[turn], row_sems.at[turn])
        for copy in across:
            copy.start()
        for copy in across:
            copy.wait_recv()
        column_tiles[turn, s] = total_of([row_tiles[turn, i] for i in range(groups)])
        along = slab_exchange(column_tiles.at[turn], column_sems.at[turn])
        for copy in along:
            copy.start()
        for copy in along:
            copy.wait_recv()
        copies += across + along
        volumes = total_of([column_tiles[turn, i] for i in range(slabs)])
        if turn == 0:
            target = volumes[:, 0:1]
        above = (volumes > target) & (lane >= 1) & (lane < TRIALS)
        count = jnp.sum(jnp.where(above, 1.0, 0.0), axis=1, keepdims=True)
        low = low + count[0:1] * width
    shrink = jnp.exp(-0.5 * (low + 0.5 * width))
    for cell in range(cells):
        design = design_ref[cell]
        factor = jnp.sqrt(jnp.maximum(sensitivities[cell], 0.0) / measures[cell]) * shrink
        new_ref[cell] = jnp.minimum(
            jnp.maximum(design * factor, jnp.maximum(design - MOVE_LIMIT, 0.0)),
            jnp.minimum(design + MOVE_LIMIT, 1.0),
        )

    @pl.when(s > 0)
    def _():
        plane_copy().wait_send()

    for copy in copies + weight_copies:
        copy.wait_send()
    for layer in range(cells):
        for d in range(1, groups):
            form_copy(layer, d).wait_send()
    design_halo("wait_send", 1)
    grad_halo("wait_send", 1)


def local(slabs, groups, design, mode_shapes, eigenvalues):
    cells, rows, depth = design.shape
    modes, node_rows = mode_shapes.shape[0], mode_shapes.shape[3]
    f32 = jnp.float32
    ext = pltpu.VMEM((cells + 2 * MARGIN, rows + 2 * PAD, depth), f32)
    forms = pltpu.VMEM((groups, cells, 2, rows, depth), f32)
    dma = pltpu.SemaphoreType.DMA
    vmem = pl.BlockSpec(memory_space=pltpu.VMEM)
    return pl.pallas_call(
        functools.partial(kernel, slabs, groups),
        out_shape=[jax.ShapeDtypeStruct(design.shape, f32)] * 2,
        in_specs=[vmem, vmem, pl.BlockSpec(memory_space=pltpu.SMEM)],
        out_specs=[vmem, vmem],
        scratch_shapes=[
            ext, ext,
            pltpu.VMEM((modes, 3, node_rows, depth), f32),
            forms, forms,
            pltpu.VMEM((groups, 8, depth), f32),
            pltpu.VMEM((128, depth), f32),
            pltpu.VMEM((2, groups, 8, 128), f32),
            pltpu.VMEM((2, slabs, 8, 128), f32),
            pltpu.VMEM((3, cells * rows, depth), f32),
            dma((2, len(DIRECTIONS))), dma((2, len(DIRECTIONS))), dma((2,)),
            dma((2, cells, groups)), dma((2, groups)), dma((2, 2, groups)), dma((2, 2, slabs)),
        ],
        compiler_params=pltpu.CompilerParams(
            collective_id=0, has_side_effects=True, vmem_limit_bytes=32 * 1024 * 1024
        ),
    )(design, mode_shapes, eigenvalues)


def solution(mesh):
    in_specs = (P("slab", "mode", None), P("mode", None, "slab", None, None), P("mode"))
    out_specs = (P("slab", "mode", None), P("slab", "mode", None))
    body = functools.partial(local, mesh.shape["slab"], mesh.shape["mode"])
    return jax.shard_map(body, mesh=mesh, in_specs=in_specs, out_specs=out_specs, check_vma=False)
```

```python
import functools
import math

import jax
import jax.numpy as jnp
from jax import lax
from jax.experimental import pallas as pl
from jax.experimental.pallas import tpu as pltpu
from jax.sharding import PartitionSpec as P

FR = 3
BISECT = 12
KS_SHARP = 2.0
PENALTY = 3.0
FLOOR_MODULUS = 0.001
MOVE_LIMIT = 0.2
POISSON = 0.3
LEVEL_LOW = -14.0
LEVEL_HIGH = 14.0

MARGIN = FR - 1
PAD = 8
STEPS = BISECT // 2
TRIALS = 2**STEPS
LAME = POISSON / ((1.0 + POISSON) * (1.0 - 2.0 * POISSON))
SHEAR = 0.5 / (1.0 + POISSON)
MESH = pl.DeviceIdType.MESH
DIRECT_LIMIT = 64
DIRECTIONS = [(dx, dy) for dx in (-1, 0, 1) for dy in (-1, 0, 1) if (dx, dy) != (0, 0)]


def edge_weight(position, count):
    total = jnp.zeros(position.shape, jnp.float32)
    for offset in range(-MARGIN, MARGIN + 1):
        inside = (position + offset >= 0) & (position + offset < count)
        total = total + jnp.where(inside, float(FR - abs(offset)), 0.0)
    return total


def axis_tables(position, count):
    measure = jnp.zeros(position.shape, jnp.float32)
    for offset in range(-MARGIN, MARGIN + 1):
        moved = position + offset
        inside = (moved >= 0) & (moved < count)
        weight = jnp.maximum(edge_weight(moved, count), 1.0)
        measure = measure + jnp.where(inside, float(FR - abs(offset)) / weight, 0.0)
    return edge_weight(position, count), measure


def filtered(ext, cells, rows, depth):
    lane = lax.broadcasted_iota(jnp.int32, (rows, depth), 1)
    results = []
    for cell in range(cells):
        along = None
        for offset in range(2 * MARGIN + 1):
            term = float(FR - abs(offset - MARGIN)) * ext[cell + offset]
            along = term if along is None else along + term
        total = None
        for offset in range(-MARGIN, MARGIN + 1):
            moved = pltpu.roll(along, (-offset) % (rows + 2 * PAD), 0) if offset else along
            term = float(FR - abs(offset)) * moved[PAD : PAD + rows]
            total = term if total is None else total + term
        value = float(FR) * total
        for offset in range(1, MARGIN + 1):
            after = jnp.where(lane < depth - offset, pltpu.roll(total, depth - offset, 1), 0.0)
            before = jnp.where(lane >= offset, pltpu.roll(total, offset, 1), 0.0)
            value = value + float(FR - offset) * (after + before)
        results.append(value)
    return results


def plane_parts(view, row, sub, node_rows, depth):
    after = row + sub
    following = view(pl.multiple_of(jnp.minimum(after, node_rows - 8), 8), 8)
    following = jnp.where(after < node_rows, following, jnp.zeros_like(following))
    value = jnp.concatenate([view(row, sub), following], 0)
    lane = lax.broadcasted_iota(jnp.int32, value.shape, 1)
    lifted = jnp.where(lane < depth - 1, pltpu.roll(value, depth - 1, 1), 0.0)
    parts = {}
    for z, base in ((0, value + lifted), (1, lifted - value)):
        above = pltpu.roll(base, sub + 7, 0)[:sub]
        parts[0, z] = base[:sub] + above
        parts[1, z] = above - base[:sub]
    return parts


def total_of(terms):
    result = terms[0]
    for term in terms[1:]:
        result = result + term
    return result


def energies(first, second):
    h = []
    for a, b in zip(first, second):
        h.append({(p, *key): (b[key] - a[key] if p else a[key] + b[key]) for p in (0, 1) for key in a})
    u, v, w = h
    sq = lambda value: value * value
    squares = [{key: sq(value) for key, value in comp.items()} for comp in h]
    su, sv, sw = squares
    q1 = su[1, 0, 0] + sv[0, 1, 0] + sw[0, 0, 1]
    q2 = total_of([su[1, 1, 0], su[1, 0, 1], sv[1, 1, 0], sv[0, 1, 1], sw[1, 0, 1], sw[0, 1, 1]])
    q3 = su[1, 1, 1] + sv[1, 1, 1] + sw[1, 1, 1]
    m0 = su[0, 0, 0] + sv[0, 0, 0] + sw[0, 0, 0]
    m1 = q1 + total_of([su[0, 1, 0], su[0, 0, 1], sv[1, 0, 0], sv[0, 0, 1], sw[1, 0, 0], sw[0, 1, 0]])
    m2 = q2 + total_of([su[0, 1, 1], sv[1, 0, 1], sw[1, 1, 0]])
    div0 = sq(u[1, 0, 0] + v[0, 1, 0] + w[0, 0, 1])
    div1 = sq(v[1, 1, 0] + w[1, 0, 1]) + sq(u[1, 1, 0] + w[0, 1, 1]) + sq(u[1, 0, 1] + v[0, 1, 1])
    cut0 = sq(u[0, 1, 0] + v[1, 0, 0]) + sq(u[0, 0, 1] + w[1, 0, 0]) + sq(v[0, 0, 1] + w[0, 1, 0])
    cut1 = sq(u[0, 1, 1] + v[1, 0, 1]) + sq(u[0, 1, 1] + w[1, 1, 0]) + sq(v[1, 0, 1] + w[1, 1, 0])
    stiff = (
        (LAME / 16.0) * div0
        + (SHEAR / 16.0) * (2.0 * q1 + cut0)
        + (LAME / 48.0) * div1
        + (SHEAR / 48.0) * (3.0 * q2 + cut1)
        + ((LAME + 4.0 * SHEAR) / 144.0) * q3
    )
    mass = (1.0 / 64.0) * m0 + (1.0 / 192.0) * m1 + (1.0 / 576.0) * m2 + (1.0 / 1728.0) * q3
    return stiff, mass


def kernel(
    slabs, groups,
    design_hbm, shapes_hbm, eig_ref, sens_ref, new_ref,
    design_ref, shapes_ref, design_ext, grad_ext, plane, outgoing, incoming, weight_tiles, partial,
    row_tiles, column_tiles, trial_rows,
    load_sems, design_sems, grad_sems, plane_sems, form_sems, weight_sems, row_sems, column_sems,
):
    cells, rows, depth = design_ref.shape
    modes, node_rows = shapes_ref.shape[0], shapes_ref.shape[3]
    total_x, total_rows = cells * slabs, rows * groups
    s, m = lax.axis_index("slab"), lax.axis_index("mode")
    me, devices = s * groups + m, slabs * groups
    direct = devices <= DIRECT_LIMIT
    sub = 16 if rows % 16 == 0 else 8

    load_shapes = pltpu.make_async_copy(shapes_hbm, shapes_ref, load_sems.at[0])
    load_design = pltpu.make_async_copy(design_hbm, design_ref, load_sems.at[1])
    load_shapes.start()
    load_design.start()
    design_ext[...] = jnp.zeros_like(design_ext)
    grad_ext[...] = jnp.zeros_like(grad_ext)

    barrier = pltpu.get_barrier_semaphore()

    def greet(x, y):
        pl.semaphore_signal(barrier, inc=1, device_id=(x, y), device_id_type=MESH)

    if direct:
        expected = devices - 1
        for d in range(1, devices):
            peer = lax.rem(me + d, devices)
            greet(peer // groups, lax.rem(peer, groups))
    else:
        expected = (groups - 1) + (slabs - 1)
        for d in range(1, groups):
            greet(s, lax.rem(m + d, groups))
        for d in range(1, slabs):
            greet(lax.rem(s + d, slabs), m)
        for dx, dy in DIRECTIONS:
            if dx and dy:
                fits = (s + dx >= 0) & (s + dx < slabs) & (m + dy >= 0) & (m + dy < groups)
                expected = expected + fits.astype(jnp.int32)

                @pl.when(fits)
                def _():
                    greet(s + dx, m + dy)

    def plane_copy(piece):
        if piece == groups:
            start, count = m * rows, PAD
        elif piece == 0:
            start, count = m * rows + PAD, rows - PAD
        else:
            start, count = lax.rem(m + piece, groups) * rows, rows
        at = pl.ds(pl.multiple_of(start, 8), count)
        return pltpu.make_async_remote_copy(
            src_ref=shapes_ref.at[:, :, 0, at], dst_ref=plane.at[:, :, at],
            send_sem=plane_sems.at[0, piece], recv_sem=plane_sems.at[1, piece],
            device_id=(s - 1, m), device_id_type=MESH,
        )

    pieces = list(range(1, groups)) + [groups] + ([0] if rows > PAD else [])

    def each_piece(action):
        here = s < slabs - 1 if action == "wait_recv" else s > 0

        def run(some):
            @pl.when(here)
            def _():
                for piece in some:
                    getattr(plane_copy(piece), action)()

        return run

    def halo(source, x_off, y_off, target, sems, number):
        dx, dy = DIRECTIONS[number]
        x_from, x_count, x_to = {
            1: (cells - MARGIN, MARGIN, 0), -1: (0, MARGIN, MARGIN + cells), 0: (0, cells, MARGIN)}[dx]
        y_from, y_count, y_to = {
            1: (rows - PAD, PAD, 0), -1: (0, PAD, PAD + rows), 0: (0, rows, PAD)}[dy]
        return pltpu.make_async_remote_copy(
            src_ref=source.at[pl.ds(x_off + x_from, x_count), pl.ds(y_off + y_from, y_count)],
            dst_ref=target.at[pl.ds(x_to, x_count), pl.ds(y_to, y_count)],
            send_sem=sems.at[0, number], recv_sem=sems.at[1, number],
            device_id=(s + dx, m + dy), device_id_type=MESH,
        )

    def each_halo(source, x_off, y_off, target, sems, action, sign):
        for number, (dx, dy) in enumerate(DIRECTIONS):
            x, y = s + sign * dx, m + sign * dy

            @pl.when((x >= 0) & (x < slabs) & (y >= 0) & (y < groups))
            def _():
                getattr(halo(source, x_off, y_off, target, sems, number), action)()

    design_halo = functools.partial(each_halo, design_ref, 0, 0, design_ext, design_sems)
    grad_halo = functools.partial(each_halo, grad_ext, MARGIN, PAD, grad_ext, grad_sems)

    weights = [jnp.exp(-KS_SHARP * jnp.full((8, depth), eig_ref[k])) for k in range(modes)]
    weight_tiles[m] = total_of(weights)

    def mode_exchange(buffer, sems):
        return [
            pltpu.make_async_remote_copy(
                src_ref=buffer.at[m], dst_ref=buffer.at[m],
                send_sem=sems.at[0, d], recv_sem=sems.at[1, d],
                device_id=(s, lax.rem(m + d, groups)), device_id_type=MESH,
            )
            for d in range(1, groups)
        ]

    def slab_exchange(buffer, sems):
        return [
            pltpu.make_async_remote_copy(
                src_ref=buffer.at[s], dst_ref=buffer.at[s],
                send_sem=sems.at[0, d], recv_sem=sems.at[1, d],
                device_id=(lax.rem(s + d, slabs), m), device_id_type=MESH,
            )
            for d in range(1, slabs)
        ]

    def all_exchange(buffer, sems):
        copies = []
        for d in range(1, devices):
            peer = lax.rem(me + d, devices)
            copies.append(
                pltpu.make_async_remote_copy(
                    src_ref=buffer.at[me], dst_ref=buffer.at[me],
                    send_sem=sems.at[0], recv_sem=sems.at[1],
                    device_id=(peer // groups, lax.rem(peer, groups)), device_id_type=MESH,
                )
            )
        others = buffer.at[pl.ds(0, devices - 1)]
        waits = [pltpu.make_async_copy(others, others, sems.at[i]) for i in range(2)]
        return copies, waits

    weight_copies = mode_exchange(weight_tiles, weight_sems)

    def node_view(mode, comp, layer):
        if layer == cells:
            return lambda row, count: plane[mode, comp, pl.ds(row, count), :]
        return lambda row, count: shapes_ref[mode, comp, layer, pl.ds(row, count), :]

    def layer_forms(layer, group):
        def step(number, carry):
            row = pl.multiple_of(group * rows + number * sub, 8)
            stiff_sum = mass_sum = None
            for mode in range(modes):
                first, second = [
                    [plane_parts(node_view(mode, comp, at), row, sub, node_rows, depth) for comp in range(3)]
                    for at in (layer, layer + 1)
                ]
                stiff, mass = energies(first, second)
                weight = weights[mode][0:1]
                stiff = weight * stiff
                mass = (weight * eig_ref[mode]) * mass
                stiff_sum = stiff if mode == 0 else stiff_sum + stiff
                mass_sum = mass if mode == 0 else mass_sum + mass
            at = pl.multiple_of(number * sub, 8)
            outgoing[group, layer, 0, pl.ds(at, sub), :] = stiff_sum
            outgoing[group, layer, 1, pl.ds(at, sub), :] = mass_sum
            return carry

        lax.fori_loop(0, rows // sub, step, 0)

    def form_copy(layer, d):
        group = lax.rem(m + d, groups)
        return pltpu.make_async_remote_copy(
            src_ref=outgoing.at[group, layer], dst_ref=incoming.at[d, layer],
            send_sem=form_sems.at[0, layer, d], recv_sem=form_sems.at[1, layer, d],
            device_id=(s, group), device_id_type=MESH,
        )

    order = list(range(1, groups)) + [0]
    x_tables = [axis_tables(jnp.full((1, depth), s * cells + i, jnp.int32), total_x) for i in range(cells)]
    y_tables = axis_tables(m * rows + lax.broadcasted_iota(jnp.int32, (rows, depth), 0), total_rows)
    z_tables = axis_tables(lax.broadcasted_iota(jnp.int32, (1, depth), 1), depth)
    spans = [x[0] * (y_tables[0] * z_tables[0]) for x in x_tables]
    measures = [x[1] * (y_tables[1] * z_tables[1]) for x in x_tables]

    @pl.when(s == slabs - 1)
    def _():
        plane[...] = jnp.zeros_like(plane)

    load_shapes.wait()
    for layer in range(cells - 1):
        for d in order:
            layer_forms(layer, lax.rem(m + d, groups))
    load_design.wait()
    pl.semaphore_wait(barrier, expected)

    each_piece("start")(pieces)
    for layer in range(cells - 1):
        for d in range(1, groups):
            form_copy(layer, d).start()
    for copy in weight_copies:
        copy.start()
    design_halo("start", 1)
    design_ext[MARGIN : MARGIN + cells, PAD : PAD + rows, :] = design_ref[...]
    design_halo("wait_recv", -1)
    densities = [f / span for f, span in zip(filtered(design_ext, cells, rows, depth), spans)]

    waiting = list(pieces)
    for number, d in enumerate(order):
        ready = len(waiting) if d == 0 else (2 if number == 0 else 1)
        each_piece("wait_recv")(waiting[:ready])
        waiting = waiting[ready:]
        layer_forms(cells - 1, lax.rem(m + d, groups))
        if d:
            form_copy(cells - 1, d).start()

    for copy in weight_copies:
        copy.wait_recv()
    weight_total = total_of([weight_tiles[i] for i in range(groups)])[0:1]
    for cell in range(cells):
        stiff, mass = outgoing[m, cell, 0], outgoing[m, cell, 1]
        for d in range(1, groups):
            form_copy(cell, d).wait_recv()
            stiff = stiff + incoming[d, cell, 0]
            mass = mass + incoming[d, cell, 1]
        slope = PENALTY * (1.0 - FLOOR_MODULUS) * densities[cell] * densities[cell]
        gradient = (slope * stiff - mass) / weight_total
        grad_ext[MARGIN + cell, PAD : PAD + rows, :] = gradient / spans[cell]
    grad_halo("start", 1)
    grad_halo("wait_recv", -1)
    sensitivities = filtered(grad_ext, cells, rows, depth)

    lowers, uppers, scales = [], [], []
    for cell in range(cells):
        sensitivity, measure = sensitivities[cell], measures[cell]
        sens_ref[cell] = sensitivity
        design = design_ref[cell]
        scales.append(design * jnp.sqrt(jnp.maximum(sensitivity, 0.0) / measure) * measure)
        lowers.append(jnp.maximum(design - MOVE_LIMIT, 0.0) * measure)
        uppers.append(jnp.minimum(design + MOVE_LIMIT, 1.0) * measure)
    lower, upper, scale = [jnp.concatenate(parts, 0) for parts in (lowers, uppers, scales)]
    trial_rows[1] = lower
    trial_rows[2] = upper

    def folded(value):
        return jnp.sum(value, axis=0, keepdims=True)

    lane = lax.broadcasted_iota(jnp.int32, (1, 128), 1)
    low = jnp.full((1, 1), LEVEL_LOW, jnp.float32)
    target = None
    width = LEVEL_HIGH - LEVEL_LOW
    sends = [copy.wait_send for copy in weight_copies]
    for turn in range(2):
        width = width / TRIALS
        trial_rows[0] = scale * jnp.exp(-0.5 * low)
        for trial in range(0, TRIALS, 8):
            lines = []
            for number in range(trial, trial + 8):
                if number == 0:
                    lines.append(folded(total_of(densities)))
                    continue
                factor = math.exp(-0.5 * width * number)
                lines.append(folded(jnp.minimum(jnp.maximum(trial_rows[0] * factor, trial_rows[1]), trial_rows[2])))
            partial[trial : trial + 8, :] = jnp.concatenate(lines, 0)
        if turn == 0:
            partial[TRIALS:, :] = jnp.zeros((partial.shape[0] - TRIALS, depth), jnp.float32)
        summed = lax.dot_general(
            jnp.ones((8, depth), jnp.float32), partial[...], (((1,), (1,)), ((), ())),
            precision=lax.Precision.HIGHEST, preferred_element_type=jnp.float32,
        )
        if direct:
            row_tiles[turn, me] = summed[0:1]
            copies, waits = all_exchange(row_tiles.at[turn], row_sems.at[turn])
            for copy in copies:
                copy.start()
            waits[1].wait()
            sends.append(waits[0].wait)
            volumes = total_of([row_tiles[turn, i] for i in range(devices)])
        else:
            row_tiles[turn, m] = summed[0:1]
            across = mode_exchange(row_tiles.at[turn], row_sems.at[turn])
            for copy in across:
                copy.start()
            for copy in across:
                copy.wait_recv()
            column_tiles[turn, s] = total_of([row_tiles[turn, i] for i in range(groups)])
            along = slab_exchange(column_tiles.at[turn], column_sems.at[turn])
            for copy in along:
                copy.start()
            for copy in along:
                copy.wait_recv()
            sends += [copy.wait_send for copy in across + along]
            volumes = total_of([column_tiles[turn, i] for i in range(slabs)])
        if turn == 0:
            target = volumes[:, 0:1]
        above = (volumes > target) & (lane >= 1) & (lane < TRIALS)
        count = jnp.sum(jnp.where(above, 1.0, 0.0), axis=1, keepdims=True)
        low = low + count * width
    shrink = jnp.exp(-0.5 * (low + 0.5 * width))
    for cell in range(cells):
        design = design_ref[cell]
        factor = jnp.sqrt(jnp.maximum(sensitivities[cell], 0.0) / measures[cell]) * shrink
        new_ref[cell] = jnp.minimum(
            jnp.maximum(design * factor, jnp.maximum(design - MOVE_LIMIT, 0.0)),
            jnp.minimum(design + MOVE_LIMIT, 1.0),
        )

    each_piece("wait_send")(pieces)
    for wait in sends:
        wait()
    for layer in range(cells):
        for d in range(1, groups):
            form_copy(layer, d).wait_send()
    design_halo("wait_send", 1)
    grad_halo("wait_send", 1)


def local(slabs, groups, design, mode_shapes, eigenvalues):
    cells, rows, depth = design.shape
    modes, node_rows = mode_shapes.shape[0], mode_shapes.shape[3]
    f32 = jnp.float32
    ext = pltpu.VMEM((cells + 2 * MARGIN, rows + 2 * PAD, depth), f32)
    forms = pltpu.VMEM((groups, cells, 2, rows, depth), f32)
    dma = pltpu.SemaphoreType.DMA
    vmem, hbm = [pl.BlockSpec(memory_space=space) for space in (pltpu.VMEM, pltpu.HBM)]
    devices = slabs * groups
    direct = devices <= DIRECT_LIMIT
    return pl.pallas_call(
        functools.partial(kernel, slabs, groups),
        out_shape=[jax.ShapeDtypeStruct(design.shape, f32)] * 2,
        in_specs=[hbm, hbm, pl.BlockSpec(memory_space=pltpu.SMEM)],
        out_specs=[vmem, vmem],
        scratch_shapes=[
            pltpu.VMEM(design.shape, f32), pltpu.VMEM(mode_shapes.shape, f32),
            ext, ext,
            pltpu.VMEM((modes, 3, node_rows, depth), f32),
            forms, forms,
            pltpu.VMEM((groups, 8, depth), f32),
            pltpu.VMEM((128, depth), f32),
            pltpu.VMEM((2, devices if direct else groups, 1, 128), f32),
            pltpu.VMEM((2, slabs, 1, 128), f32),
            pltpu.VMEM((3, cells * rows, depth), f32),
            dma((2,)), dma((2, len(DIRECTIONS))), dma((2, len(DIRECTIONS))), dma((2, groups + 1)),
            dma((2, cells, groups)), dma((2, groups)), dma((2, 2) if direct else (2, 2, groups)), dma((2, 2, slabs)),
        ],
        compiler_params=pltpu.CompilerParams(
            collective_id=0, has_side_effects=True, vmem_limit_bytes=32 * 1024 * 1024
        ),
    )(design, mode_shapes, eigenvalues)


def solution(mesh):
    in_specs = (P("slab", "mode", None), P("mode", None, "slab", None, None), P("mode"))
    out_specs = (P("slab", "mode", None), P("slab", "mode", None))
    body = functools.partial(local, mesh.shape["slab"], mesh.shape["mode"])
    return jax.shard_map(body, mesh=mesh, in_specs=in_specs, out_specs=out_specs, check_vma=False)
```

```python
import functools
import math

import jax
import jax.numpy as jnp
from jax import lax
from jax.experimental import pallas as pl
from jax.experimental.pallas import tpu as pltpu
from jax.sharding import PartitionSpec as P

FR = 3
BISECT = 12
KS_SHARP = 2.0
PENALTY = 3.0
FLOOR_MODULUS = 0.001
MOVE_LIMIT = 0.2
POISSON = 0.3
LEVEL_LOW = -14.0
LEVEL_HIGH = 14.0

MARGIN = FR - 1
PAD = 8
STEPS = BISECT // 2
TRIALS = 2**STEPS
LAME = POISSON / ((1.0 + POISSON) * (1.0 - 2.0 * POISSON))
SHEAR = 0.5 / (1.0 + POISSON)
MESH = pl.DeviceIdType.MESH
DIRECT_LIMIT = 64
DIRECTIONS = [(dx, dy) for dx in (-1, 0, 1) for dy in (-1, 0, 1) if (dx, dy) != (0, 0)]


def edge_weight(position, count):
    total = jnp.zeros(position.shape, jnp.float32)
    for offset in range(-MARGIN, MARGIN + 1):
        inside = (position + offset >= 0) & (position + offset < count)
        total = total + jnp.where(inside, float(FR - abs(offset)), 0.0)
    return total


def axis_tables(position, count):
    measure = jnp.zeros(position.shape, jnp.float32)
    for offset in range(-MARGIN, MARGIN + 1):
        moved = position + offset
        inside = (moved >= 0) & (moved < count)
        weight = jnp.maximum(edge_weight(moved, count), 1.0)
        measure = measure + jnp.where(inside, float(FR - abs(offset)) / weight, 0.0)
    return edge_weight(position, count), measure


def filtered(ext, cells, rows, depth):
    lane = lax.broadcasted_iota(jnp.int32, (rows, depth), 1)
    results = []
    for cell in range(cells):
        along = None
        for offset in range(2 * MARGIN + 1):
            term = float(FR - abs(offset - MARGIN)) * ext[cell + offset]
            along = term if along is None else along + term
        total = None
        for offset in range(-MARGIN, MARGIN + 1):
            moved = pltpu.roll(along, (-offset) % (rows + 2 * PAD), 0) if offset else along
            term = float(FR - abs(offset)) * moved[PAD : PAD + rows]
            total = term if total is None else total + term
        value = float(FR) * total
        for offset in range(1, MARGIN + 1):
            after = jnp.where(lane < depth - offset, pltpu.roll(total, depth - offset, 1), 0.0)
            before = jnp.where(lane >= offset, pltpu.roll(total, offset, 1), 0.0)
            value = value + float(FR - offset) * (after + before)
        results.append(value)
    return results


def plane_parts(view, row, sub, node_rows, depth):
    after = row + sub
    following = view(pl.multiple_of(jnp.minimum(after, node_rows - 8), 8), 8)
    following = jnp.where(after < node_rows, following, jnp.zeros_like(following))
    value = jnp.concatenate([view(row, sub), following], 0)
    lane = lax.broadcasted_iota(jnp.int32, value.shape, 1)
    lifted = jnp.where(lane < depth - 1, pltpu.roll(value, depth - 1, 1), 0.0)
    parts = {}
    for z, base in ((0, value + lifted), (1, lifted - value)):
        above = pltpu.roll(base, sub + 7, 0)[:sub]
        parts[0, z] = base[:sub] + above
        parts[1, z] = above - base[:sub]
    return parts


def total_of(terms):
    result = terms[0]
    for term in terms[1:]:
        result = result + term
    return result


def energies(first, second):
    h = []
    for a, b in zip(first, second):
        h.append({(p, *key): (b[key] - a[key] if p else a[key] + b[key]) for p in (0, 1) for key in a})
    u, v, w = h
    sq = lambda value: value * value
    squares = [{key: sq(value) for key, value in comp.items()} for comp in h]
    su, sv, sw = squares
    q1 = su[1, 0, 0] + sv[0, 1, 0] + sw[0, 0, 1]
    q2 = total_of([su[1, 1, 0], su[1, 0, 1], sv[1, 1, 0], sv[0, 1, 1], sw[1, 0, 1], sw[0, 1, 1]])
    q3 = su[1, 1, 1] + sv[1, 1, 1] + sw[1, 1, 1]
    m0 = su[0, 0, 0] + sv[0, 0, 0] + sw[0, 0, 0]
    m1 = q1 + total_of([su[0, 1, 0], su[0, 0, 1], sv[1, 0, 0], sv[0, 0, 1], sw[1, 0, 0], sw[0, 1, 0]])
    m2 = q2 + total_of([su[0, 1, 1], sv[1, 0, 1], sw[1, 1, 0]])
    div0 = sq(u[1, 0, 0] + v[0, 1, 0] + w[0, 0, 1])
    div1 = sq(v[1, 1, 0] + w[1, 0, 1]) + sq(u[1, 1, 0] + w[0, 1, 1]) + sq(u[1, 0, 1] + v[0, 1, 1])
    cut0 = sq(u[0, 1, 0] + v[1, 0, 0]) + sq(u[0, 0, 1] + w[1, 0, 0]) + sq(v[0, 0, 1] + w[0, 1, 0])
    cut1 = sq(u[0, 1, 1] + v[1, 0, 1]) + sq(u[0, 1, 1] + w[1, 1, 0]) + sq(v[1, 0, 1] + w[1, 1, 0])
    stiff = (
        (LAME / 16.0) * div0
        + (SHEAR / 16.0) * (2.0 * q1 + cut0)
        + (LAME / 48.0) * div1
        + (SHEAR / 48.0) * (3.0 * q2 + cut1)
        + ((LAME + 4.0 * SHEAR) / 144.0) * q3
    )
    mass = (1.0 / 64.0) * m0 + (1.0 / 192.0) * m1 + (1.0 / 576.0) * m2 + (1.0 / 1728.0) * q3
    return stiff, mass


def kernel(
    slabs, groups,
    design_hbm, shapes_hbm, eig_ref, sens_ref, new_ref,
    design_ref, shapes_ref, design_ext, grad_ext, plane, outgoing, incoming, weight_tiles, partial,
    row_tiles, column_tiles, trial_rows,
    load_sems, design_sems, grad_sems, plane_sems, form_sems, weight_sems, row_sems, column_sems,
):
    cells, rows, depth = design_ref.shape
    modes, node_rows = shapes_ref.shape[0], shapes_ref.shape[3]
    total_x, total_rows = cells * slabs, rows * groups
    s, m = lax.axis_index("slab"), lax.axis_index("mode")
    me, devices = s * groups + m, slabs * groups
    direct = devices <= DIRECT_LIMIT
    xs = [s] + [jnp.where(s + d >= slabs, s + d - slabs, s + d) for d in range(1, slabs)]
    ys = [m] + [jnp.where(m + d >= groups, m + d - groups, m + d) for d in range(1, groups)]
    far_first = sorted(range(slabs), key=lambda d: abs(2 * d - slabs))
    peers = [(xs[dx], ys[dy]) for dx in far_first for dy in range(groups) if dx or dy]
    sub = 16 if rows % 16 == 0 else 8

    load_shapes = pltpu.make_async_copy(shapes_hbm, shapes_ref, load_sems.at[0])
    load_design = pltpu.make_async_copy(design_hbm, design_ref, load_sems.at[1])
    load_shapes.start()
    load_design.start()
    design_ext[...] = jnp.zeros_like(design_ext)
    grad_ext[...] = jnp.zeros_like(grad_ext)

    barrier = pltpu.get_barrier_semaphore()

    def greet(x, y):
        pl.semaphore_signal(barrier, inc=1, device_id=(x, y), device_id_type=MESH)

    if direct:
        expected = devices - 1
        for peer in peers:
            greet(*peer)
    else:
        expected = (groups - 1) + (slabs - 1)
        for d in range(1, groups):
            greet(s, ys[d])
        for d in range(1, slabs):
            greet(xs[d], m)
        for dx, dy in DIRECTIONS:
            if dx and dy:
                fits = (s + dx >= 0) & (s + dx < slabs) & (m + dy >= 0) & (m + dy < groups)
                expected = expected + fits.astype(jnp.int32)

                @pl.when(fits)
                def _():
                    greet(s + dx, m + dy)

    def plane_copy(piece):
        if piece == groups:
            start, count = m * rows, PAD
        elif piece == 0:
            start, count = m * rows + PAD, rows - PAD
        else:
            start, count = ys[piece] * rows, rows
        at = pl.ds(pl.multiple_of(start, 8), count)
        return pltpu.make_async_remote_copy(
            src_ref=shapes_ref.at[:, :, 0, at], dst_ref=plane.at[:, :, at],
            send_sem=plane_sems.at[0, piece], recv_sem=plane_sems.at[1, piece],
            device_id=(s - 1, m), device_id_type=MESH,
        )

    pieces = list(range(1, groups)) + [groups] + ([0] if rows > PAD else [])

    def each_piece(action):
        here = s < slabs - 1 if action == "wait_recv" else s > 0

        def run(some):
            @pl.when(here)
            def _():
                for piece in some:
                    getattr(plane_copy(piece), action)()

        return run

    def halo(source, x_off, y_off, target, sems, number):
        dx, dy = DIRECTIONS[number]
        x_from, x_count, x_to = {
            1: (cells - MARGIN, MARGIN, 0), -1: (0, MARGIN, MARGIN + cells), 0: (0, cells, MARGIN)}[dx]
        y_from, y_count, y_to = {
            1: (rows - PAD, PAD, 0), -1: (0, PAD, PAD + rows), 0: (0, rows, PAD)}[dy]
        return pltpu.make_async_remote_copy(
            src_ref=source.at[pl.ds(x_off + x_from, x_count), pl.ds(y_off + y_from, y_count)],
            dst_ref=target.at[pl.ds(x_to, x_count), pl.ds(y_to, y_count)],
            send_sem=sems.at[0, number], recv_sem=sems.at[1, number],
            device_id=(s + dx, m + dy), device_id_type=MESH,
        )

    def each_halo(source, x_off, y_off, target, sems, action, sign):
        for number, (dx, dy) in enumerate(DIRECTIONS):
            x, y = s + sign * dx, m + sign * dy

            @pl.when((x >= 0) & (x < slabs) & (y >= 0) & (y < groups))
            def _():
                getattr(halo(source, x_off, y_off, target, sems, number), action)()

    design_halo = functools.partial(each_halo, design_ref, 0, 0, design_ext, design_sems)
    grad_halo = functools.partial(each_halo, grad_ext, MARGIN, PAD, grad_ext, grad_sems)

    weights = [jnp.exp(-KS_SHARP * jnp.full((8, depth), eig_ref[k])) for k in range(modes)]
    weight_tiles[m] = total_of(weights)

    def mode_exchange(buffer, sems):
        return [
            pltpu.make_async_remote_copy(
                src_ref=buffer.at[m], dst_ref=buffer.at[m],
                send_sem=sems.at[0, d], recv_sem=sems.at[1, d],
                device_id=(s, ys[d]), device_id_type=MESH,
            )
            for d in range(1, groups)
        ]

    def slab_exchange(buffer, sems):
        return [
            pltpu.make_async_remote_copy(
                src_ref=buffer.at[s], dst_ref=buffer.at[s],
                send_sem=sems.at[0, d], recv_sem=sems.at[1, d],
                device_id=(xs[d], m), device_id_type=MESH,
            )
            for d in range(1, slabs)
        ]

    def all_exchange(buffer, sems):
        copies = []
        for peer in peers:
            copies.append(
                pltpu.make_async_remote_copy(
                    src_ref=buffer.at[me], dst_ref=buffer.at[me],
                    send_sem=sems.at[0], recv_sem=sems.at[1],
                    device_id=peer, device_id_type=MESH,
                )
            )
        others = buffer.at[pl.ds(0, devices - 1)]
        waits = [pltpu.make_async_copy(others, others, sems.at[i]) for i in range(2)]
        return copies, waits

    weight_copies = mode_exchange(weight_tiles, weight_sems)

    def node_view(mode, comp, layer):
        if layer == cells:
            return lambda row, count: plane[mode, comp, pl.ds(row, count), :]
        return lambda row, count: shapes_ref[mode, comp, layer, pl.ds(row, count), :]

    def layer_forms(layer, group):
        def step(number, carry):
            row = pl.multiple_of(group * rows + number * sub, 8)
            stiff_sum = mass_sum = None
            for mode in range(modes):
                first, second = [
                    [plane_parts(node_view(mode, comp, at), row, sub, node_rows, depth) for comp in range(3)]
                    for at in (layer, layer + 1)
                ]
                stiff, mass = energies(first, second)
                weight = weights[mode][0:1]
                stiff = weight * stiff
                mass = (weight * eig_ref[mode]) * mass
                stiff_sum = stiff if mode == 0 else stiff_sum + stiff
                mass_sum = mass if mode == 0 else mass_sum + mass
            at = pl.multiple_of(number * sub, 8)
            outgoing[group, layer, 0, pl.ds(at, sub), :] = stiff_sum
            outgoing[group, layer, 1, pl.ds(at, sub), :] = mass_sum
            return carry

        lax.fori_loop(0, rows // sub, step, 0)

    def form_copy(layer, d):
        group = ys[d]
        return pltpu.make_async_remote_copy(
            src_ref=outgoing.at[group, layer], dst_ref=incoming.at[d, layer],
            send_sem=form_sems.at[0, layer, d], recv_sem=form_sems.at[1, layer, d],
            device_id=(s, group), device_id_type=MESH,
        )

    order = list(range(1, groups)) + [0]
    x_tables = [axis_tables(jnp.full((1, depth), s * cells + i, jnp.int32), total_x) for i in range(cells)]
    y_tables = axis_tables(m * rows + lax.broadcasted_iota(jnp.int32, (rows, depth), 0), total_rows)
    z_tables = axis_tables(lax.broadcasted_iota(jnp.int32, (1, depth), 1), depth)
    spans = [x[0] * (y_tables[0] * z_tables[0]) for x in x_tables]
    measures = [x[1] * (y_tables[1] * z_tables[1]) for x in x_tables]

    @pl.when(s == slabs - 1)
    def _():
        plane[...] = jnp.zeros_like(plane)

    load_shapes.wait()
    for layer in range(cells - 1):
        for d in order:
            layer_forms(layer, ys[d])
    load_design.wait()
    pl.semaphore_wait(barrier, expected)

    each_piece("start")(pieces)
    for layer in range(cells - 1):
        for d in range(1, groups):
            form_copy(layer, d).start()
    for copy in weight_copies:
        copy.start()
    design_halo("start", 1)
    design_ext[MARGIN : MARGIN + cells, PAD : PAD + rows, :] = design_ref[...]

    waiting = list(pieces)
    for number, d in enumerate(order):
        ready = len(waiting) if d == 0 else (2 if number == 0 else 1)
        each_piece("wait_recv")(waiting[:ready])
        waiting = waiting[ready:]
        layer_forms(cells - 1, ys[d])
        if d:
            form_copy(cells - 1, d).start()

    design_halo("wait_recv", -1)
    densities = [f / span for f, span in zip(filtered(design_ext, cells, rows, depth), spans)]
    for copy in weight_copies:
        copy.wait_recv()
    weight_total = total_of([weight_tiles[i] for i in range(groups)])[0:1]
    for cell in range(cells):
        stiff, mass = outgoing[m, cell, 0], outgoing[m, cell, 1]
        for d in range(1, groups):
            form_copy(cell, d).wait_recv()
            stiff = stiff + incoming[d, cell, 0]
            mass = mass + incoming[d, cell, 1]
        slope = PENALTY * (1.0 - FLOOR_MODULUS) * densities[cell] * densities[cell]
        gradient = (slope * stiff - mass) / weight_total
        grad_ext[MARGIN + cell, PAD : PAD + rows, :] = gradient / spans[cell]
    grad_halo("start", 1)
    grad_halo("wait_recv", -1)
    sensitivities = filtered(grad_ext, cells, rows, depth)

    lowers, uppers, scales = [], [], []
    for cell in range(cells):
        sensitivity, measure = sensitivities[cell], measures[cell]
        sens_ref[cell] = sensitivity
        design = design_ref[cell]
        scales.append(design * jnp.sqrt(jnp.maximum(sensitivity, 0.0) / measure) * measure)
        lowers.append(jnp.maximum(design - MOVE_LIMIT, 0.0) * measure)
        uppers.append(jnp.minimum(design + MOVE_LIMIT, 1.0) * measure)
    lower, upper, scale = [jnp.concatenate(parts, 0) for parts in (lowers, uppers, scales)]
    trial_rows[1] = lower
    trial_rows[2] = upper

    def folded(value):
        return jnp.sum(value, axis=0, keepdims=True)

    lane = lax.broadcasted_iota(jnp.int32, (1, 128), 1)
    low = jnp.full((1, 1), LEVEL_LOW, jnp.float32)
    target = None
    width = LEVEL_HIGH - LEVEL_LOW
    sends = [copy.wait_send for copy in weight_copies]
    for turn in range(2):
        width = width / TRIALS
        trial_rows[0] = scale * jnp.exp(-0.5 * low)
        for trial in range(0, TRIALS, 8):
            lines = []
            for number in range(trial, trial + 8):
                if number == 0:
                    lines.append(folded(total_of(densities)))
                    continue
                factor = math.exp(-0.5 * width * number)
                lines.append(folded(jnp.minimum(jnp.maximum(trial_rows[0] * factor, trial_rows[1]), trial_rows[2])))
            partial[trial : trial + 8, :] = jnp.concatenate(lines, 0)
        if turn == 0:
            partial[TRIALS:, :] = jnp.zeros((partial.shape[0] - TRIALS, depth), jnp.float32)
        summed = lax.dot_general(
            jnp.ones((8, depth), jnp.float32), partial[...], (((1,), (1,)), ((), ())),
            precision=lax.Precision.HIGHEST, preferred_element_type=jnp.float32,
        )
        if direct:
            row_tiles[turn, me] = summed[0:1]
            copies, waits = all_exchange(row_tiles.at[turn], row_sems.at[turn])
            for copy in copies:
                copy.start()
            waits[1].wait()
            sends.append(waits[0].wait)
            volumes = total_of([row_tiles[turn, i] for i in range(devices)])
        else:
            row_tiles[turn, m] = summed[0:1]
            across = mode_exchange(row_tiles.at[turn], row_sems.at[turn])
            for copy in across:
                copy.start()
            for copy in across:
                copy.wait_recv()
            column_tiles[turn, s] = total_of([row_tiles[turn, i] for i in range(groups)])
            along = slab_exchange(column_tiles.at[turn], column_sems.at[turn])
            for copy in along:
                copy.start()
            for copy in along:
                copy.wait_recv()
            sends += [copy.wait_send for copy in across + along]
            volumes = total_of([column_tiles[turn, i] for i in range(slabs)])
        if turn == 0:
            target = volumes[:, 0:1]
        above = (volumes > target) & (lane >= 1) & (lane < TRIALS)
        count = jnp.sum(jnp.where(above, 1.0, 0.0), axis=1, keepdims=True)
        low = low + count * width
    shrink = jnp.exp(-0.5 * (low + 0.5 * width))
    for cell in range(cells):
        design = design_ref[cell]
        factor = jnp.sqrt(jnp.maximum(sensitivities[cell], 0.0) / measures[cell]) * shrink
        new_ref[cell] = jnp.minimum(
            jnp.maximum(design * factor, jnp.maximum(design - MOVE_LIMIT, 0.0)),
            jnp.minimum(design + MOVE_LIMIT, 1.0),
        )

    each_piece("wait_send")(pieces)
    for wait in sends:
        wait()
    for layer in range(cells):
        for d in range(1, groups):
            form_copy(layer, d).wait_send()
    design_halo("wait_send", 1)
    grad_halo("wait_send", 1)


def local(slabs, groups, design, mode_shapes, eigenvalues):
    cells, rows, depth = design.shape
    modes, node_rows = mode_shapes.shape[0], mode_shapes.shape[3]
    f32 = jnp.float32
    ext = pltpu.VMEM((cells + 2 * MARGIN, rows + 2 * PAD, depth), f32)
    forms = pltpu.VMEM((groups, cells, 2, rows, depth), f32)
    dma = pltpu.SemaphoreType.DMA
    vmem, hbm = [pl.BlockSpec(memory_space=space) for space in (pltpu.VMEM, pltpu.HBM)]
    devices = slabs * groups
    direct = devices <= DIRECT_LIMIT
    return pl.pallas_call(
        functools.partial(kernel, slabs, groups),
        out_shape=[jax.ShapeDtypeStruct(design.shape, f32)] * 2,
        in_specs=[hbm, hbm, pl.BlockSpec(memory_space=pltpu.SMEM)],
        out_specs=[vmem, vmem],
        scratch_shapes=[
            pltpu.VMEM(design.shape, f32), pltpu.VMEM(mode_shapes.shape, f32),
            ext, ext,
            pltpu.VMEM((modes, 3, node_rows, depth), f32),
            forms, forms,
            pltpu.VMEM((groups, 8, depth), f32),
            pltpu.VMEM((128, depth), f32),
            pltpu.VMEM((2, devices if direct else groups, 1, 128), f32),
            pltpu.VMEM((2, slabs, 1, 128), f32),
            pltpu.VMEM((3, cells * rows, depth), f32),
            dma((2,)), dma((2, len(DIRECTIONS))), dma((2, len(DIRECTIONS))), dma((2, groups + 1)),
            dma((2, cells, groups)), dma((2, groups)), dma((2, 2) if direct else (2, 2, groups)), dma((2, 2, slabs)),
        ],
        compiler_params=pltpu.CompilerParams(
            collective_id=0, has_side_effects=True, vmem_limit_bytes=32 * 1024 * 1024
        ),
    )(design, mode_shapes, eigenvalues)


def solution(mesh):
    in_specs = (P("slab", "mode", None), P("mode", None, "slab", None, None), P("mode"))
    out_specs = (P("slab", "mode", None), P("slab", "mode", None))
    body = functools.partial(local, mesh.shape["slab"], mesh.shape["mode"])
    return jax.shard_map(body, mesh=mesh, in_specs=in_specs, out_specs=out_specs, check_vma=False)
```
